1024 devices in a mesh: grp: 8 (over y), exp: 32 (over z, core), hs: 4 (over x).
Axes of the slice: x: 4, y: 8, z: 16, core: 2. Of those that a mesh axis runs over, the one named last changes fastest.
Arguments:
- tokens: bfloat16 [4096, 3584], P(('grp', 'exp'), 'hs'), may hold values from -6 to 6
- grad_out: bfloat16 [4096, 3584], P(('grp', 'exp'), 'hs'), may hold values from -6 to 6
- gates: float32 [4096, 8], P(('grp', 'exp')), may hold values from 0.05 to 1
- routes: int32 [4096, 8], P(('grp', 'exp')), may hold values from 0 to 127, as said below
- kept: int32 [4096, 8], P(('grp', 'exp')), may hold values from 0 to 1, as said below
- w_gate: bfloat16 [256, 3584, 512], P(('grp', 'exp'), 'hs'), may hold values from -0.09375 to 0.09375
- w_up: bfloat16 [256, 3584, 512], P(('grp', 'exp'), 'hs'), may hold values from -0.09375 to 0.09375
- w_down: bfloat16 [256, 512, 3584], P(('grp', 'exp'), None, 'hs'), may hold values from -0.1875 to 0.1875
Outputs:
- input_grad: bfloat16 [4096, 3584], P(('grp', 'exp'), 'hs')
The draws below stay inside these ranges and needn't reach their ends.
Inputs may be any that keep to these rules, and one draw needn't show every extreme that they name: `routes`: each row names 8 different experts, all inside 4 of the 8 groups; group j holds experts j * 16 to (j + 1) * 16 - 1. Take the tokens of all devices with one exp index e, the rows (g * 32 + e) * 16 to (g * 32 + e + 1) * 16 - 1 for every g: their routes with kept = 1 to any one expert number at most 16, and for every e some expert gets exactly 16.
All inputs are finite; a program needn't handle non-finite values.
Results may differ from the reference program's by a relative error of at most 0.012.
Values may be sent and summed in bfloat16 or wider, within the bound.
No kernel may reach another device: no remote copies, remote signals or barrier semaphores. Data moves between devices by JAX's collectives and lax.ppermute only.
A program may use at most 32 MiB of HBM per device.

```python
import jax
import jax.numpy as jnp
from jax import lax

D = 3584
HID = 1024
TOK_DEV = 16
EXP_GROUP = 16
EXPERTS = 128
GROUP_TOP = 4
TOP = 8
TOKENS = 4096
CAP = 16
N_GRP = 8
N_EXP = 32


def route_draw(key):
    keys = jax.random.split(key, 4)
    hot_expert = jax.random.randint(keys[0], (), 0, EXPERTS, dtype=jnp.int32)
    hot_group = hot_expert // EXP_GROUP
    group_ids = jnp.arange(N_GRP, dtype=jnp.int32)
    expert_ids = jnp.arange(EXPERTS, dtype=jnp.int32)
    forced_rows = (CAP + N_GRP - 1) // N_GRP
    local_row = jnp.arange(TOKENS, dtype=jnp.int32) % TOK_DEV
    forced = (local_row < forced_rows)[:, None]
    group_score = jax.random.randint(keys[1], (TOKENS, N_GRP), 0, 2 ** 20, dtype=jnp.int32) * N_GRP + group_ids
    group_score = jnp.where(forced & (group_ids == hot_group), 2 ** 30, group_score)
    _, group_pick = lax.top_k(group_score, GROUP_TOP)
    allowed = jnp.any(group_pick[:, :, None] == (expert_ids // EXP_GROUP)[None, None, :], axis=1)
    bias = jax.random.randint(keys[2], (EXPERTS,), 0, 2 ** 21, dtype=jnp.int32)
    noise = jax.random.randint(keys[3], (TOKENS, EXPERTS), 0, 2 ** 20, dtype=jnp.int32)
    score = (bias[None, :] + noise) * EXPERTS + expert_ids
    score = jnp.where(allowed, score, -1)
    score = jnp.where(forced & (expert_ids == hot_expert), 2 ** 30 + 1, score)
    _, routes = lax.top_k(score, TOP)
    routes = routes.astype(jnp.int32)
    per_column = N_GRP * TOK_DEV * TOP
    flat = routes.reshape(N_GRP, N_EXP, TOK_DEV * TOP).transpose(1, 0, 2).reshape(N_EXP, per_column)
    onehot = (flat[:, :, None] == expert_ids[None, None, :]).astype(jnp.int32)
    ranks = jnp.cumsum(onehot, axis=1) - 1
    own_rank = jnp.sum(ranks * onehot, axis=2)
    keep = (own_rank < CAP).astype(jnp.int32)
    kept = keep.reshape(N_EXP, N_GRP, TOK_DEV * TOP).transpose(1, 0, 2).reshape(TOKENS, TOP)
    return (routes, kept)


def draw_routes(key, part):
    shared = route_draw(key)
    return shared[0]


def draw_kept(key, part):
    shared = route_draw(key)
    return shared[1]


def levels(stream_key, extent, cuts, smallest, high):
    factor_of, own = 1.0, jax.random.fold_in(stream_key, 6)
    for axis_at, parts in cuts:
        steps = jnp.exp(jax.random.uniform(jax.random.fold_in(own, axis_at), (parts,), jnp.float32, smallest / len(cuts), high / len(cuts)))
        factor_of = factor_of * jnp.repeat(steps, extent[axis_at] // parts).reshape([-1 if axis == axis_at else 1 for axis in range(len(extent))])
    return factor_of


def normal_values(key, shape, spread, most, shards=(), held_as=jnp.bfloat16):
    drawn = jax.random.normal(key, shape, jnp.float32) * spread
    if len(shards) > 0:
        drawn = levels(key, shape, shards, -0.22, 0.18) * drawn
    return jnp.clip(drawn, min=-most, max=most).astype(held_as)


def setup_inputs(seed: int = 0) -> dict:
    streams_of = jax.random.split(jax.random.key(seed), 9)
    return {
        "tokens": normal_values(streams_of[0], (TOKENS, D), 1.0, 6.0, ((0, 256), (1, 4))),
        "grad_out": normal_values(streams_of[1], (TOKENS, D), 1.0, 6.0, ((0, 256), (1, 4))),
        "gates": jnp.clip(0.05 + 0.95 * jax.random.uniform(streams_of[2], (TOKENS, TOP), jnp.float32) ** levels(streams_of[2], (TOKENS, TOP), ((0, 256),), -0.2, 0.2), 0.05, 1.0),
        "routes": draw_routes(jax.random.fold_in(streams_of[8], 71), 0),
        "kept": draw_kept(jax.random.fold_in(streams_of[8], 71), 0),
        "w_gate": normal_values(streams_of[5], (2 * EXPERTS, D, HID // 2), D ** -0.5, 0.09375, ((0, 256), (1, 4))),
        "w_up": normal_values(streams_of[6], (2 * EXPERTS, D, HID // 2), D ** -0.5, 0.09375, ((0, 256), (1, 4))),
        "w_down": normal_values(streams_of[7], (2 * EXPERTS, HID // 2, D), HID ** -0.5, 0.1875, ((0, 256), (2, 4))),
    }


def backprop(gate_pre, up_pre, hidden_grad):
    sigma = jax.nn.sigmoid(gate_pre)
    slope = sigma * (1.0 + gate_pre * (1.0 - sigma))
    gate_grad = (hidden_grad * up_pre * slope).astype(jnp.bfloat16)
    up_grad = (hidden_grad * gate_pre * sigma).astype(jnp.bfloat16)
    return gate_grad, up_grad


def reference(tokens, grad_out, gates, routes, kept, w_gate, w_up, w_down):
    weight = lax.optimization_barrier(gates.astype(jnp.bfloat16)).astype(jnp.float32)
    most_rows = N_EXP * CAP
    contract = (((1,), (1,)), ((), ()))
    slot_numbers = jnp.arange(most_rows, dtype=jnp.int32)

    def expert_step(total, expert):
        chosen = (routes == expert) & (kept == 1)
        route_weight = jnp.sum(jnp.where(chosen, weight, 0.0), axis=1)
        used = jnp.any(chosen, axis=1)
        used_count = jnp.sum(used.astype(jnp.int32))
        row_index = jnp.nonzero(used, size=most_rows, fill_value=0)[0].astype(jnp.int32)
        valid = slot_numbers < used_count
        rows_x = tokens[row_index]
        rows_dy = grad_out[row_index].astype(jnp.float32)
        rows_w = jnp.where(valid, route_weight[row_index], 0.0)
        start = (2 * expert).astype(jnp.int32)
        gate_blk = lax.dynamic_slice_in_dim(w_gate, start, 2, 0)
        up_blk = lax.dynamic_slice_in_dim(w_up, start, 2, 0)
        down_blk = lax.dynamic_slice_in_dim(w_down, start, 2, 0)
        gate_mat = jnp.concatenate([gate_blk[0], gate_blk[1]], axis=1)
        up_mat = jnp.concatenate([up_blk[0], up_blk[1]], axis=1)
        down_mat = jnp.concatenate([down_blk[0], down_blk[1]], axis=0)
        gate_pre = jnp.dot(rows_x, gate_mat, preferred_element_type=jnp.float32)
        up_pre = jnp.dot(rows_x, up_mat, preferred_element_type=jnp.float32)
        dout = (rows_w[:, None] * rows_dy).astype(jnp.bfloat16)
        hidden_grad = lax.dot_general(dout, down_mat, contract, preferred_element_type=jnp.float32)
        gate_grad, up_grad = backprop(gate_pre, up_pre, hidden_grad)
        input_part = lax.dot_general(gate_grad, gate_mat, contract, preferred_element_type=jnp.float32)
        input_part = input_part + lax.dot_general(up_grad, up_mat, contract, preferred_element_type=jnp.float32)
        return total.at[row_index].add(input_part), None

    total = jnp.zeros((TOKENS, D), jnp.float32)
    total, _ = lax.scan(expert_step, total, jnp.arange(EXPERTS, dtype=jnp.int32))
    return total.astype(jnp.bfloat16)
```

```python
import jax
import jax.numpy as jnp
from jax import lax
from jax.sharding import Mesh, PartitionSpec as P

BF = jnp.bfloat16
F32 = jnp.float32
LAST = (((1,), (1,)), ((), ()))


def backprop(gate_pre, up_pre, hidden_grad):
    sigma = jax.nn.sigmoid(gate_pre)
    slope = sigma * (1.0 + gate_pre * (1.0 - sigma))
    gate_grad = (hidden_grad * up_pre * slope).astype(BF)
    up_grad = (hidden_grad * gate_pre * sigma).astype(BF)
    return (gate_grad, up_grad)


def swap_cores(rows):
    return lax.ppermute(rows, "core", [(0, 1), (1, 0)])


def spread(rows):
    copies = jnp.broadcast_to(rows[None], (lax.axis_size("grp"),) + rows.shape)
    return lax.all_to_all(copies, "grp", 0, 0, tiled=True).reshape(-1, rows.shape[1])


def sum_over_hs(parts):
    n_hs = lax.axis_size("hs")
    pieces = parts.astype(BF).reshape(n_hs, -1, parts.shape[1])
    return jnp.sum(lax.all_to_all(pieces, "hs", 0, 0, tiled=True).astype(F32), axis=0)


def shards(tokens, grad_out, gates, routes, kept, w_gate, w_up, w_down):
    n_grp = lax.axis_size("grp")
    n_z = lax.axis_size("z")
    experts = n_grp * n_z
    tok_rows, width = tokens.shape
    capacity = 2 * n_grp * tok_rows * routes.shape[1] // experts
    gate_w, up_w, down_w = w_gate[0], w_up[0], w_down[0]
    hidden = gate_w.shape[1]

    expert_ids = jnp.arange(experts, dtype=jnp.int32)
    chosen = (routes[:, :, None] == expert_ids[None, None, :]) & (kept[:, :, None] == 1)
    table = jnp.sum(jnp.where(chosen, gates[:, :, None], 0.0), axis=1).astype(BF)

    packed = spread(jnp.concatenate([tokens, table], axis=1))
    all_tokens = packed[:, :width]
    all_grads = spread(grad_out)
    group_cols = lax.dynamic_slice_in_dim(
        packed[:, width:], lax.axis_index("grp") * n_z, n_z, 1
    ).astype(F32)
    present = (group_cols != 0.0).astype(F32)
    position = jnp.cumsum(present, axis=0) - 1.0
    slot_ids = jnp.arange(capacity, dtype=F32)
    placing = present.T[:, None, :] * (position.T[:, None, :] == slot_ids[None, :, None]).astype(F32)
    placing_low = placing.astype(BF).reshape(n_z * capacity, -1)
    slot_weight = jnp.sum(placing * group_cols.T[:, None, :], axis=2).reshape(-1, 1)

    slot_x = jnp.dot(placing_low, all_tokens, preferred_element_type=F32).astype(BF)
    slot_dy = jnp.dot(placing_low, all_grads, preferred_element_type=F32)
    slot_grad = (slot_weight * slot_dy).astype(BF)

    def dispatch(rows):
        mine = lax.all_to_all(
            rows.reshape(n_z, capacity, width), "z", 0, 0, tiled=True
        ).reshape(-1, width)
        return jnp.concatenate([mine, swap_cores(mine)], axis=0)

    rows_x = dispatch(slot_x)
    rows_grad = dispatch(slot_grad)
    gate_part = jnp.dot(rows_x, gate_w, preferred_element_type=F32)
    up_part = jnp.dot(rows_x, up_w, preferred_element_type=F32)
    pre = sum_over_hs(jnp.concatenate([gate_part, up_part], axis=1))
    hidden_part = lax.dot_general(rows_grad, down_w, LAST, preferred_element_type=F32)
    hidden_sum = sum_over_hs(hidden_part)
    gate_grad, up_grad = backprop(pre[:, :hidden], pre[:, hidden:], hidden_sum)
    both = lax.all_gather(
        jnp.concatenate([gate_grad, up_grad], axis=1), "hs", axis=0, tiled=True
    )
    input_part = lax.dot_general(both[:, :hidden], gate_w, LAST, preferred_element_type=F32)
    input_part = input_part + lax.dot_general(
        both[:, hidden:], up_w, LAST, preferred_element_type=F32
    )
    half = n_z * capacity
    mine = input_part[:half] + swap_cores(input_part[half:].astype(BF)).astype(F32)
    returned = lax.all_to_all(
        mine.astype(BF).reshape(n_z, capacity, width), "z", 0, 0, tiled=True
    ).reshape(-1, width)
    token_rows = lax.dot_general(
        placing_low, returned, (((0,), (0,)), ((), ())), preferred_element_type=F32
    )
    back_rows = lax.all_to_all(
        token_rows.astype(BF).reshape(n_grp, tok_rows, width), "grp", 0, 0, tiled=True
    )
    return jnp.sum(back_rows.astype(F32), axis=0).astype(BF)


def solution(mesh):
    n_grp, n_exp, n_hs = mesh.devices.shape
    chips = Mesh(
        mesh.devices.reshape(n_grp, n_exp // 2, 2, n_hs), ("grp", "z", "core", "hs")
    )
    rows = ("grp", "z", "core")
    placed = (
        P(rows, "hs"),
        P(rows, "hs"),
        P(rows, None),
        P(rows, None),
        P(rows, None),
        P(rows, "hs", None),
        P(rows, "hs", None),
        P(rows, None, "hs"),
    )
    return jax.shard_map(
        shards, mesh=chips, in_specs=placed, out_specs=P(rows, "hs"), check_vma=False
    )
```

```python
import jax
import jax.numpy as jnp
from jax import lax
from jax.sharding import Mesh, PartitionSpec as P

BF = jnp.bfloat16
F32 = jnp.float32
LAST = (((1,), (1,)), ((), ()))
CORES = [(0, 1), (1, 0)]


def backprop(gate_pre, up_pre, hidden_grad):
    sigma = jax.nn.sigmoid(gate_pre)
    slope = sigma * (1.0 + gate_pre * (1.0 - sigma))
    gate_grad = (hidden_grad * up_pre * slope).astype(BF)
    up_grad = (hidden_grad * gate_pre * sigma).astype(BF)
    return (gate_grad, up_grad)


def spread(rows, axis):
    copies = jnp.broadcast_to(rows[None], (lax.axis_size(axis),) + rows.shape)
    return lax.all_to_all(copies, axis, 0, 0, tiled=True).reshape(-1, rows.shape[1])


def sum_by_permutes(parts, axis):
    n, me = lax.axis_size(axis), lax.axis_index(axis)
    pieces = parts.reshape(n, -1, parts.shape[1])
    total = lax.dynamic_index_in_dim(pieces, me, 0, keepdims=False).astype(F32)
    for step in range(1, n):
        piece = lax.dynamic_index_in_dim(pieces, lax.rem(me + step, n), 0, keepdims=False)
        got = lax.ppermute(piece, axis, [(i, (i + step) % n) for i in range(n)])
        total = total + got.astype(F32)
    return total


def sum_by_exchange(parts, axis):
    pieces = parts.reshape(lax.axis_size(axis), -1, parts.shape[1])
    return jnp.sum(lax.all_to_all(pieces, axis, 0, 0, tiled=True).astype(F32), axis=0)


def shards(tokens, grad_out, gates, routes, kept, w_gate, w_up, w_down):
    n_grp = lax.axis_size("grp")
    n_z = lax.axis_size("z")
    experts = n_grp * n_z
    tok_rows, width = tokens.shape
    capacity = 2 * n_grp * tok_rows * routes.shape[1] // experts
    gate_w, up_w, down_w = w_gate[0], w_up[0], w_down[0]

    gate_o, up_o, down_o = (lax.ppermute(w, "core", CORES) for w in (gate_w, up_w, down_w))

    expert_ids = jnp.arange(experts, dtype=jnp.int32)
    chosen = (routes[:, :, None] == expert_ids[None, None, :]) & (kept[:, :, None] == 1)
    table = jnp.sum(jnp.where(chosen, gates[:, :, None], 0.0), axis=1).astype(BF)

    packed = spread(jnp.concatenate([tokens, table], axis=1), "grp")
    all_tokens = packed[:, :width]
    group_cols = lax.dynamic_slice_in_dim(
        packed[:, width:], lax.axis_index("grp") * n_z, n_z, 1
    ).astype(F32)
    present = (group_cols != 0.0).astype(F32)
    position = jnp.cumsum(present, axis=0) - 1.0
    slot_ids = jnp.arange(capacity, dtype=F32)
    placing = present.T[:, None, :] * (position.T[:, None, :] == slot_ids[None, :, None]).astype(F32)
    placing_low = placing.astype(BF).reshape(n_z * capacity, -1)
    slot_weight = jnp.sum(placing * group_cols.T[:, None, :], axis=2).reshape(-1, 1)

    def dispatch(rows):
        return lax.all_to_all(
            rows.reshape(n_z, capacity, width), "z", 0, 0, tiled=True
        ).reshape(-1, width)

    slot_x = jnp.dot(placing_low, all_tokens, preferred_element_type=F32).astype(BF)
    slot_x, grad_out = lax.optimization_barrier((slot_x, grad_out))
    rows_x = dispatch(slot_x)
    all_grads = lax.all_gather(grad_out, "grp", axis=0, tiled=True)
    slot_dy = jnp.dot(placing_low, all_grads, preferred_element_type=F32)
    slot_grad = (slot_weight * slot_dy).astype(BF)
    rows_x, slot_grad = lax.optimization_barrier((rows_x, slot_grad))
    rows_grad = dispatch(slot_grad)
    pre_parts = jnp.concatenate(
        [
            jnp.dot(rows_x, w, preferred_element_type=F32).astype(BF)
            for w in (gate_w, gate_o, up_w, up_o)
        ],
        axis=1,
    )
    pre = sum_by_permutes(pre_parts, "hs")
    hidden = pre.shape[1] // 2
    grad_parts = jnp.concatenate(
        [
            lax.dot_general(rows_grad, w, LAST, preferred_element_type=F32).astype(BF)
            for w in (down_w, down_o)
        ],
        axis=1,
    )
    hidden_sum = sum_by_exchange(grad_parts, "hs")
    gate_grad, up_grad = backprop(pre[:, :hidden], pre[:, hidden:], hidden_sum)
    both = spread(jnp.concatenate([gate_grad, up_grad], axis=1), "hs")
    half = hidden // 2
    mine = sum(
        lax.dot_general(
            both[:, i * half : (i + 1) * half], w, LAST, preferred_element_type=F32
        )
        for i, w in enumerate((gate_w, gate_o, up_w, up_o))
    )
    returned = dispatch(mine.astype(BF))
    token_rows = lax.dot_general(
        placing_low, returned, (((0,), (0,)), ((), ())), preferred_element_type=F32
    )
    back_rows = lax.all_to_all(
        token_rows.astype(BF).reshape(n_grp, tok_rows, width), "grp", 0, 0, tiled=True
    )
    return jnp.sum(back_rows.astype(F32), axis=0).astype(BF)


def solution(mesh):
    n_grp, n_exp, n_hs = mesh.devices.shape
    chips = Mesh(
        mesh.devices.reshape(n_grp, n_exp // 2, 2, n_hs), ("grp", "z", "core", "hs")
    )
    rows = ("grp", "z", "core")
    placed = (
        P(rows, "hs"),
        P(rows, "hs"),
        P(rows, None),
        P(rows, None),
        P(rows, None),
        P(rows, "hs", None),
        P(rows, "hs", None),
        P(rows, None, "hs"),
    )
    return jax.shard_map(
        shards, mesh=chips, in_specs=placed, out_specs=P(rows, "hs"), check_vma=False
    )
```

```python
import functools

import jax
import jax.numpy as jnp
from jax import lax
from jax.experimental import pallas as pl
from jax.experimental.pallas import tpu as pltpu
from jax.sharding import Mesh, PartitionSpec as P

BF = jnp.bfloat16
F32 = jnp.float32
LAST = (((1,), (1,)), ((), ()))
CORES = [(0, 1), (1, 0)]
LANES = 128
VMEM_BYTES = 60 * 1024 * 1024


def backprop(gate_pre, up_pre, hidden_grad):
    sigma = jax.nn.sigmoid(gate_pre)
    slope = sigma * (1.0 + gate_pre * (1.0 - sigma))
    gate_grad = (hidden_grad * up_pre * slope).astype(BF)
    up_grad = (hidden_grad * gate_pre * sigma).astype(BF)
    return (gate_grad, up_grad)


def dot(a, b):
    return jnp.dot(a, b, preferred_element_type=F32)


def dot_last(a, b):
    return lax.dot_general(a, b, LAST, preferred_element_type=F32)


def iota(shape, axis):
    return lax.broadcasted_iota(jnp.int32, shape, axis)


def whole(shape):
    return pl.BlockSpec(shape, lambda step: (0,) * len(shape))


def local_call(kernel, out_shape, flops, *operands, grid=1, specs=None, out_specs=None, scratch=()):
    outs = out_shape if isinstance(out_shape, tuple) else (out_shape,)
    size = sum(v.size * v.dtype.itemsize for v in operands + outs)
    if out_specs is None:
        out_specs = tuple(whole(v.shape) for v in outs)
    return pl.pallas_call(
        kernel,
        out_shape=out_shape,
        grid=(grid,),
        in_specs=specs or [whole(v.shape) for v in operands],
        out_specs=out_specs if isinstance(out_shape, tuple) else out_specs[0],
        scratch_shapes=scratch,
        compiler_params=pltpu.CompilerParams(vmem_limit_bytes=VMEM_BYTES),
        cost_estimate=pl.CostEstimate(flops=flops, bytes_accessed=size, transcendentals=0),
    )(*operands)


def pack_kernel(n_z, tokens, grads, gates, routes, kept, out):
    n_grp, tok_rows, _ = out.shape
    width = tokens.shape[1]
    place = iota((tok_rows, LANES), 1) == iota((tok_rows, LANES), 0) + lax.axis_index("grp") * tok_rows
    place = place.astype(F32).astype(BF)
    low = lambda v: v.astype(F32).astype(BF)
    used = low(kept[...])
    weight = dot(low(gates[...]) * used, place)
    expert = jnp.where(dot(used, place) > 0.5, dot(low(routes[...]), place), -1.0)
    ids = iota((n_grp * n_z, LANES), 0).astype(F32)
    table = jnp.zeros((n_grp * n_z, LANES), F32)
    for k in range(weight.shape[0]):
        table = table + jnp.where(expert[k : k + 1] == ids, weight[k : k + 1], 0.0)
    table = table.astype(BF)
    if n_z < tok_rows:
        out[:, :, 2 * width :] = jnp.zeros((n_grp, tok_rows, LANES), BF)
    for g in range(n_grp):
        out[g, :, :width] = tokens[...]
        out[g, :, width : 2 * width] = grads[...]
        out[g, :n_z, 2 * width :] = table[g * n_z : (g + 1) * n_z]


def place_kernel(n_z, capacity, packed, slot_x, slot_grad, placing):
    n_grp, tok_rows, _ = packed.shape
    width = slot_x.shape[1]
    n_tok = n_grp * tok_rows
    cols = jnp.zeros((tok_rows, LANES), F32)
    for g in range(n_grp):
        cols = cols + packed[g, :, 2 * width :].astype(F32)
    present = cols != 0.0
    before = (iota((LANES, LANES), 0) < iota((LANES, LANES), 1)).astype(F32).astype(BF)
    position = jnp.where(present, dot(present.astype(F32).astype(BF), before), -1.0)
    slot = iota((capacity, LANES), 0).astype(F32)
    weights = []
    for q in range(n_z):
        here = position[q : q + 1] == slot
        weights.append(jnp.sum(jnp.where(here, cols[q : q + 1], 0.0), axis=1, keepdims=True))
        placing[q * capacity : (q + 1) * capacity, :] = here.astype(F32).astype(BF)
    weight = jnp.concatenate(weights, axis=0)
    chosen = placing[:, :n_tok]
    rows = packed[:, :, :width].reshape(n_tok, width)
    slot_x[...] = dot(chosen, rows).astype(BF)
    rows = packed[:, :, width : 2 * width].reshape(n_tok, width)
    slot_grad[...] = (weight * dot(chosen, rows)).astype(BF)


def pre_kernel(n_hs, rows, w0, w1, w2, w3, *refs):
    outs, hold = refs[:n_hs], refs[n_hs]
    half = w0.shape[1]
    count = outs[0].shape[0]
    for i, w in enumerate((w0, w1, w2, w3)):
        hold[:, i * half : (i + 1) * half] = dot(rows[...], w[...]).astype(BF)
    me = lax.axis_index("hs")
    for step, out in enumerate(outs):
        start = pl.multiple_of(lax.rem(me + step, n_hs) * count, count)
        out[...] = hold[pl.ds(start, count), :]


def hidden_kernel(rows, w0, w1, out):
    n_hs, count, _ = out.shape
    step, block = pl.program_id(0), w0.shape[0]
    half = block * pl.num_programs(0)
    for i, w in enumerate((w0, w1)):
        part = dot_last(rows[...], w[...]).astype(BF)
        here = pl.ds(pl.multiple_of(step * block + i * half, block), block)
        for p in range(n_hs):
            out[p, :, here] = part[p * count : (p + 1) * count]


def act_kernel(hidden_parts, *refs):
    pre_parts, out = refs[:-1], refs[-1]
    n_hs, _, hidden = hidden_parts.shape
    total = lambda parts: functools.reduce(lambda a, b: a + b, [v.astype(F32) for v in parts])
    gate_pre = total([p[:, :hidden] for p in pre_parts])
    up_pre = total([p[:, hidden:] for p in pre_parts])
    hidden_grad = total([hidden_parts[i] for i in range(n_hs)])
    gate_grad, up_grad = backprop(gate_pre, up_pre, hidden_grad)
    for i in range(n_hs):
        out[i, :, :hidden] = gate_grad
        out[i, :, hidden:] = up_grad


def input_kernel(both, w0, w1, w2, w3, out, total):
    n_hs, count, _ = both.shape
    step, block = pl.program_id(0), w0.shape[1]
    half = block * pl.num_programs(0)

    @pl.when(step == 0)
    def _():
        total[...] = jnp.zeros(total.shape, F32)

    for i, w in enumerate((w0, w1, w2, w3)):
        here = pl.ds(pl.multiple_of(step * block + i * half, block), block)
        total[...] += dot_last(both[:, :, here].reshape(n_hs * count, block), w[...])

    @pl.when(step == pl.num_programs(0) - 1)
    def _():
        out[...] = total[...].astype(BF)


def shards(tokens, grad_out, gates, routes, kept, w_gate, w_up, w_down):
    n_grp, n_z, n_hs = (lax.axis_size(axis) for axis in ("grp", "z", "hs"))
    tok_rows, width = tokens.shape
    capacity = 2 * tok_rows * routes.shape[1] // n_z
    total = n_z * capacity
    gate_w, up_w, down_w = w_gate[0], w_up[0], w_down[0]
    half = gate_w.shape[1]
    shape = lambda *dims: jax.ShapeDtypeStruct(dims, BF)

    gate_o, up_o, down_o = (lax.ppermute(w, "core", CORES) for w in (gate_w, up_w, down_w))

    def exchange(blocks, axis):
        return lax.all_to_all(blocks, axis, 0, 0, tiled=True)

    def dispatch(rows):
        return exchange(rows.reshape(n_z, capacity, width), "z").reshape(total, width)

    packed = local_call(
        functools.partial(pack_kernel, n_z),
        shape(n_grp, tok_rows, 2 * width + LANES),
        10**6,
        tokens,
        grad_out,
        gates.T,
        routes.T,
        kept.T,
    )
    packed = exchange(packed, "grp")
    slot_x, slot_grad, placing = local_call(
        functools.partial(place_kernel, n_z, capacity),
        (shape(total, width), shape(total, width), shape(total, LANES)),
        4 * total * LANES * width,
        packed,
    )
    rows_x = dispatch(slot_x)
    rows_x, slot_grad, gate_o, up_o, down_o = lax.optimization_barrier(
        (rows_x, slot_grad, gate_o, up_o, down_o)
    )
    rows_grad = dispatch(slot_grad)
    pieces = local_call(
        functools.partial(pre_kernel, n_hs),
        (shape(total // n_hs, 4 * half),) * n_hs,
        8 * total * width * half,
        rows_x,
        gate_w,
        gate_o,
        up_w,
        up_o,
        scratch=[pltpu.VMEM((total, 4 * half), BF)],
    )
    pre_parts = [pieces[0]] + [
        lax.ppermute(pieces[step], "hs", [(i, (i + step) % n_hs) for i in range(n_hs)])
        for step in range(1, n_hs)
    ]
    rows_grad, *pre_parts = lax.optimization_barrier((rows_grad, *pre_parts))
    down_spec = pl.BlockSpec((half // 2, width), lambda step: (step, 0))
    hidden_parts = local_call(
        hidden_kernel,
        shape(n_hs, total // n_hs, 2 * half),
        4 * total * width * half,
        rows_grad,
        down_w,
        down_o,
        grid=2,
        specs=[whole(rows_grad.shape), down_spec, down_spec],
    )
    hidden_parts = exchange(hidden_parts, "hs")
    both = local_call(
        act_kernel,
        shape(n_hs, total // n_hs, 4 * half),
        20 * total * half,
        hidden_parts,
        *pre_parts,
    )
    both = exchange(both, "hs")
    mine = local_call(
        input_kernel,
        shape(total, width),
        8 * total * width * half,
        both,
        gate_w,
        gate_o,
        up_w,
        up_o,
        grid=2,
        specs=[whole(both.shape)]
        + [pl.BlockSpec((width, half // 2), lambda step: (0, step))] * 4,
        scratch=[pltpu.VMEM((total, width), F32)],
    )
    returned = dispatch(mine)
    token_rows = lax.dot_general(
        placing[:, : n_grp * tok_rows],
        returned,
        (((0,), (0,)), ((), ())),
        preferred_element_type=F32,
    )
    back_rows = exchange(token_rows.astype(BF).reshape(n_grp, tok_rows, width), "grp")
    return jnp.sum(back_rows.astype(F32), axis=0).astype(BF)


def solution(mesh):
    n_grp, n_exp, n_hs = mesh.devices.shape
    chips = Mesh(
        mesh.devices.reshape(n_grp, n_exp // 2, 2, n_hs), ("grp", "z", "core", "hs")
    )
    rows = ("grp", "z", "core")
    placed = (
        P(rows, "hs"),
        P(rows, "hs"),
        P(rows, None),
        P(rows, None),
        P(rows, None),
        P(rows, "hs", None),
        P(rows, "hs", None),
        P(rows, None, "hs"),
    )
    return jax.shard_map(
        shards, mesh=chips, in_specs=placed, out_specs=P(rows, "hs"), check_vma=False
    )
```

```python
import functools

import jax
import jax.numpy as jnp
from jax import lax
from jax.experimental import pallas as pl
from jax.experimental.pallas import tpu as pltpu
from jax.sharding import Mesh, PartitionSpec as P

BF = jnp.bfloat16
F32 = jnp.float32
LAST = (((1,), (1,)), ((), ()))
CORES = [(0, 1), (1, 0)]
LANES = 128


def backprop(gate_pre, up_pre, hidden_grad):
    sigma = jax.nn.sigmoid(gate_pre)
    slope = sigma * (1.0 + gate_pre * (1.0 - sigma))
    gate_grad = (hidden_grad * up_pre * slope).astype(BF)
    up_grad = (hidden_grad * gate_pre * sigma).astype(BF)
    return (gate_grad, up_grad)


def dot(a, b):
    return jnp.dot(a, b, preferred_element_type=F32)


def dot_last(a, b):
    return lax.dot_general(a, b, LAST, preferred_element_type=F32)


def iota(shape, axis):
    return lax.broadcasted_iota(jnp.int32, shape, axis)


def whole(shape):
    return pl.BlockSpec(shape, lambda step: (0,) * len(shape))


def local_call(kernel, out_shape, flops, *operands, grid=1, specs=None, out_specs=None, scratch=(), vmem=60):
    outs = out_shape if isinstance(out_shape, tuple) else (out_shape,)
    size = sum(v.size * v.dtype.itemsize for v in operands + outs)
    if out_specs is None:
        out_specs = tuple(whole(v.shape) for v in outs)
    return pl.pallas_call(
        kernel,
        out_shape=out_shape,
        grid=(grid,),
        in_specs=specs or [whole(v.shape) for v in operands],
        out_specs=out_specs if isinstance(out_shape, tuple) else out_specs[0],
        scratch_shapes=scratch,
        compiler_params=pltpu.CompilerParams(vmem_limit_bytes=vmem * 1024 * 1024),
        cost_estimate=pl.CostEstimate(flops=flops, bytes_accessed=size, transcendentals=0),
    )(*operands)


def select(source, rows):
    pick = (source == iota((source.shape[0], rows.shape[0]), 1)).astype(F32).astype(BF)
    return dot(pick, rows).astype(BF)


def home_rows(total, n_z, part):
    row = iota((total, 1), 0)
    return row // part % n_z * (total // n_z) + row // (part * n_z) * part + row % part


def part_rows(total, n_z, n_hs):
    row, part = iota((total, 1), 0), total // n_z // n_hs
    return row // part % n_hs * (n_z * part) + row // (total // n_z) * part + row % part


def split_rows(n_hs, hold, outs):
    count = outs[0].shape[0]
    me = lax.axis_index("hs")
    for step, out in enumerate(outs):
        start = pl.multiple_of(lax.rem(me + step, n_hs) * count, count)
        out[...] = hold[pl.ds(start, count), :]


def pack_kernel(n_z, tokens, grads, gates, routes, kept, out):
    n_grp, tok_rows, _ = out.shape
    width = tokens.shape[1]
    place = iota((tok_rows, LANES), 1) == iota((tok_rows, LANES), 0) + lax.axis_index("grp") * tok_rows
    place = place.astype(F32).astype(BF)
    low = lambda v: v.astype(F32).astype(BF)
    used = low(kept[...])
    weight = dot(low(gates[...]) * used, place)
    expert = jnp.where(dot(used, place) > 0.5, dot(low(routes[...]), place), -1.0)
    ids = iota((n_grp * n_z, LANES), 0).astype(F32)
    table = jnp.zeros((n_grp * n_z, LANES), F32)
    for k in range(weight.shape[0]):
        table = table + jnp.where(expert[k : k + 1] == ids, weight[k : k + 1], 0.0)
    table = table.astype(BF)
    if n_z < tok_rows:
        out[:, :, 2 * width :] = jnp.zeros((n_grp, tok_rows, LANES), BF)
    for g in range(n_grp):
        out[g, :, :width] = tokens[...]
        out[g, :, width : 2 * width] = grads[...]
        out[g, :n_z, 2 * width :] = table[g * n_z : (g + 1) * n_z]


def place_kernel(n_z, capacity, n_hs, packed, slot_x, placing, *refs):
    grads, hold = refs[:n_hs], refs[n_hs]
    n_grp, tok_rows, _ = packed.shape
    width = slot_x.shape[1]
    n_tok = n_grp * tok_rows
    cols = jnp.zeros((tok_rows, LANES), F32)
    for g in range(n_grp):
        cols = cols + packed[g, :, 2 * width :].astype(F32)
    present = cols != 0.0
    before = (iota((LANES, LANES), 0) < iota((LANES, LANES), 1)).astype(F32).astype(BF)
    position = jnp.where(present, dot(present.astype(F32).astype(BF), before), -1.0)
    slot = iota((capacity, LANES), 0).astype(F32)
    weights = []
    for q in range(n_z):
        here = position[q : q + 1] == slot
        weights.append(jnp.sum(jnp.where(here, cols[q : q + 1], 0.0), axis=1, keepdims=True))
        placing[q * capacity : (q + 1) * capacity, :] = here.astype(F32).astype(BF)
    weight = jnp.concatenate(weights, axis=0)
    chosen = placing[:, :n_tok]
    rows = packed[:, :, :width].reshape(n_tok, width)
    slot_x[...] = dot(chosen, rows).astype(BF)
    rows = packed[:, :, width : 2 * width].reshape(n_tok, width)
    slot_grad = (weight * dot(chosen, rows)).astype(BF)
    hold[...] = select(home_rows(n_z * capacity, n_z, capacity // n_hs), slot_grad)
    split_rows(n_hs, hold, grads)


def widen_kernel(n_z, *refs):
    pieces, out = refs[:-1], refs[-1]
    n_hs, (total, _) = len(pieces), out.shape
    part = total // n_z // n_hs
    row = iota((total, 1), 0)
    step = lax.rem(lax.axis_index("hs") - row // part % n_hs + n_hs, n_hs)
    source = step * (n_z * part) + row // (total // n_z) * part + row % part
    out[...] = select(source, jnp.concatenate([p[...] for p in pieces], axis=0))


def pre_kernel(n_hs, n_z, rows, w0, w1, w2, w3, *refs):
    outs, hold = refs[:n_hs], refs[n_hs]
    half, total = w0.shape[1], rows.shape[0]
    ordered = select(home_rows(total, n_z, total // n_z // n_hs), rows[...])
    for i, w in enumerate((w0, w1, w2, w3)):
        hold[:, i * half : (i + 1) * half] = dot(ordered, w[...]).astype(BF)
    split_rows(n_hs, hold, outs)


def act_kernel(n_z, rows, down, down_o, *refs):
    pre_parts, (out, ordered, hidden_grad) = refs[:-3], refs[-3:]
    n_hs, (total, _), half = len(pre_parts), rows.shape, down.shape[1]
    count, hidden = hidden_grad.shape
    step = pl.program_id(0)

    @pl.when(step == 0)
    def _():
        ordered[...] = select(home_rows(total, n_z, total // n_z // n_hs), rows[...])
        hidden_grad[...] = jnp.zeros(hidden_grad.shape, F32)

    block = ordered[pl.ds(pl.multiple_of(step * count, count), count), :]
    hidden_grad[:, :half] += dot_last(block, down[0])
    hidden_grad[:, half:] += dot_last(block, down_o[0])

    @pl.when(step == pl.num_programs(0) - 1)
    def _():
        add = lambda parts: functools.reduce(lambda a, b: a + b, [v.astype(F32) for v in parts])
        gate_pre = add([p[:, :hidden] for p in pre_parts])
        up_pre = add([p[:, hidden:] for p in pre_parts])
        gate_grad, up_grad = backprop(gate_pre, up_pre, hidden_grad[...])
        for i in range(n_hs):
            out[i, :, :hidden] = gate_grad
            out[i, :, hidden:] = up_grad


def input_kernel(n_z, both, w0, w1, w2, w3, out, total):
    n_hs, count, _ = both.shape
    step, block = pl.program_id(0), w0.shape[1]
    half = block * pl.num_programs(0)

    @pl.when(step == 0)
    def _():
        total[...] = jnp.zeros(total.shape, F32)

    for i, w in enumerate((w0, w1, w2, w3)):
        here = pl.ds(pl.multiple_of(step * block + i * half, block), block)
        total[...] += dot_last(both[:, :, here].reshape(n_hs * count, block), w[...])

    @pl.when(step == pl.num_programs(0) - 1)
    def _():
        order = part_rows(total.shape[0], n_z, n_hs)
        out[...] = select(order, total[...].astype(BF))


def shards(tokens, grad_out, gates, routes, kept, w_gate, w_up, w_down):
    n_grp, n_z, n_hs = (lax.axis_size(axis) for axis in ("grp", "z", "hs"))
    tok_rows, width = tokens.shape
    capacity = 2 * tok_rows * routes.shape[1] // n_z
    total = n_z * capacity
    gate_w, up_w, down_w = w_gate[0], w_up[0], w_down[0]
    half = gate_w.shape[1]
    shape = lambda *dims: jax.ShapeDtypeStruct(dims, BF)

    swap = lambda w: lax.ppermute(w, "core", CORES)
    gate_o, up_o = swap(gate_w), swap(up_w)
    down_all = lax.all_gather(down_w, "hs", axis=0, tiled=False)

    def exchange(blocks, axis):
        return lax.all_to_all(blocks, axis, 0, 0, tiled=True)

    def trade(pieces):
        return [pieces[0]] + [
            lax.ppermute(pieces[step], "hs", [(i, (i + step) % n_hs) for i in range(n_hs)])
            for step in range(1, n_hs)
        ]

    def dispatch(rows):
        return exchange(rows.reshape(n_z, capacity, width), "z").reshape(total, width)

    packed = local_call(
        functools.partial(pack_kernel, n_z),
        shape(n_grp, tok_rows, 2 * width + LANES),
        10**6,
        tokens,
        grad_out,
        gates.T,
        routes.T,
        kept.T,
    )
    packed = exchange(packed, "grp")
    slot_x, placing, *grad_pieces = local_call(
        functools.partial(place_kernel, n_z, capacity, n_hs),
        (shape(total, width), shape(total, LANES)) + (shape(total // n_hs, width),) * n_hs,
        4 * total * LANES * width,
        packed,
        scratch=[pltpu.VMEM((total, width), BF)],
        vmem=24,
    )
    rows_x = dispatch(slot_x)
    wide = local_call(
        functools.partial(widen_kernel, n_z),
        shape(total, width),
        2 * total * total * width,
        *trade(grad_pieces),
        vmem=24,
    )
    rows_x, wide, gate_o, up_o, down_all = lax.optimization_barrier(
        (rows_x, wide, gate_o, up_o, down_all)
    )
    rows_grad = dispatch(wide)
    down_o = swap(down_all)
    pieces = local_call(
        functools.partial(pre_kernel, n_hs, n_z),
        (shape(total // n_hs, 4 * half),) * n_hs,
        8 * total * width * half,
        rows_x,
        gate_w,
        gate_o,
        up_w,
        up_o,
        scratch=[pltpu.VMEM((total, 4 * half), BF)],
    )
    rows_grad, *pre_parts = lax.optimization_barrier((rows_grad, *trade(pieces)))
    down_spec = pl.BlockSpec((1, half, width), lambda step: (step, 0, 0))
    both = local_call(
        functools.partial(act_kernel, n_z),
        shape(n_hs, total // n_hs, 4 * half),
        4 * total * width * half,
        rows_grad,
        down_all,
        down_o,
        *pre_parts,
        grid=n_hs,
        specs=[whole(rows_grad.shape), down_spec, down_spec]
        + [whole(p.shape) for p in pre_parts],
        scratch=[pltpu.VMEM((total, width), BF), pltpu.VMEM((total // n_hs, 2 * half), F32)],
    )
    both = exchange(both, "hs")
    mine = local_call(
        functools.partial(input_kernel, n_z),
        shape(total, width),
        8 * total * width * half,
        both,
        gate_w,
        gate_o,
        up_w,
        up_o,
        grid=2,
        specs=[whole(both.shape)]
        + [pl.BlockSpec((width, half // 2), lambda step: (0, step))] * 4,
        scratch=[pltpu.VMEM((total, width), F32)],
    )
    returned = dispatch(mine)
    token_rows = lax.dot_general(
        placing[:, : n_grp * tok_rows],
        returned,
        (((0,), (0,)), ((), ())),
        preferred_element_type=F32,
    )
    back_rows = exchange(token_rows.astype(BF).reshape(n_grp, tok_rows, width), "grp")
    return jnp.sum(back_rows.astype(F32), axis=0).astype(BF)


def solution(mesh):
    n_grp, n_exp, n_hs = mesh.devices.shape
    chips = Mesh(
        mesh.devices.reshape(n_grp, n_exp // 2, 2, n_hs), ("grp", "z", "core", "hs")
    )
    rows = ("grp", "z", "core")
    placed = (
        P(rows, "hs"),
        P(rows, "hs"),
        P(rows, None),
        P(rows, None),
        P(rows, None),
        P(rows, "hs", None),
        P(rows, "hs", None),
        P(rows, None, "hs"),
    )
    return jax.shard_map(
        shards, mesh=chips, in_specs=placed, out_specs=P(rows, "hs"), check_vma=False
    )
```

```python
import functools

import jax
import jax.numpy as jnp
from jax import lax
from jax.experimental import pallas as pl
from jax.experimental.pallas import tpu as pltpu
from jax.sharding import Mesh, PartitionSpec as P

BF = jnp.bfloat16
F32 = jnp.float32
LAST = (((1,), (1,)), ((), ()))
CORES = [(0, 1), (1, 0)]
LANES = 128


def backprop(gate_pre, up_pre, hidden_grad):
    sigma = jax.nn.sigmoid(gate_pre)
    slope = sigma * (1.0 + gate_pre * (1.0 - sigma))
    gate_grad = (hidden_grad * up_pre * slope).astype(BF)
    up_grad = (hidden_grad * gate_pre * sigma).astype(BF)
    return (gate_grad, up_grad)


def dot(a, b):
    return jnp.dot(a, b, preferred_element_type=F32)


def dot_last(a, b):
    return lax.dot_general(a, b, LAST, preferred_element_type=F32)


def iota(shape, axis):
    return lax.broadcasted_iota(jnp.int32, shape, axis)


def local_call(kernel, out_shape, flops, vmem, held, fetched=(), scratch=()):
    outs = out_shape if isinstance(out_shape, tuple) else (out_shape,)
    size = sum(v.size * v.dtype.itemsize for v in (*held, *fetched, *outs))
    inside = pl.BlockSpec(memory_space=pltpu.VMEM)
    buffers = [pltpu.VMEM(v.shape, v.dtype) for v in fetched]
    return pl.pallas_call(
        kernel,
        out_shape=out_shape,
        in_specs=[inside] * len(held) + [pl.BlockSpec(memory_space=pltpu.HBM)] * len(fetched),
        out_specs=tuple(inside for _ in outs) if isinstance(out_shape, tuple) else inside,
        scratch_shapes=[*buffers, *[pltpu.SemaphoreType.DMA] * len(fetched), *scratch],
        compiler_params=pltpu.CompilerParams(vmem_limit_bytes=int(vmem * 1024 * 1024)),
        cost_estimate=pl.CostEstimate(flops=flops, bytes_accessed=size, transcendentals=0),
    )(*held, *fetched)


def fetch(sources, buffers, sems):
    copies = [pltpu.make_async_copy(*refs) for refs in zip(sources, buffers, sems)]
    for copy in copies:
        copy.start()
    return copies


def pack_kernel(n_z, *refs):
    out, buffers, sems = refs[5], refs[6:11], refs[11:16]
    copies = fetch(refs[:5], buffers, sems)
    tokens, grads, gates, routes, kept = buffers
    n_grp, tok_rows, _ = out.shape
    width = tokens.shape[1]
    for copy in copies:
        copy.wait()
    place = iota((tok_rows, LANES), 1) == iota((tok_rows, LANES), 0) + lax.axis_index("grp") * tok_rows
    place = place.astype(F32).astype(BF)
    low = lambda v: v.astype(F32).astype(BF)
    used = low(kept[...])
    weight = dot(low(gates[...]) * used, place)
    expert = jnp.where(dot(used, place) > 0.5, dot(low(routes[...]), place), -1.0)
    ids = iota((n_grp * n_z, LANES), 0).astype(F32)
    table = jnp.zeros((n_grp * n_z, LANES), F32)
    for k in range(weight.shape[0]):
        table = table + jnp.where(expert[k : k + 1] == ids, weight[k : k + 1], 0.0)
    table = table.astype(BF)
    if n_z < tok_rows:
        out[:, :, 2 * width :] = jnp.zeros((n_grp, tok_rows, LANES), BF)
    for g in range(n_grp):
        out[g, :, :width] = tokens[...]
        out[g, :, width : 2 * width] = grads[...]
        out[g, :n_z, 2 * width :] = table[g * n_z : (g + 1) * n_z]


def place_kernel(n_z, capacity, packed, slot_x, slot_grad, placing):
    n_grp, tok_rows, _ = packed.shape
    width = slot_x.shape[1]
    n_tok = n_grp * tok_rows
    cols = jnp.zeros((tok_rows, LANES), F32)
    for g in range(n_grp):
        cols = cols + packed[g, :, 2 * width :].astype(F32)
    present = cols != 0.0
    before = (iota((LANES, LANES), 0) < iota((LANES, LANES), 1)).astype(F32).astype(BF)
    position = jnp.where(present, dot(present.astype(F32).astype(BF), before), -1.0)
    slot = iota((capacity, LANES), 0).astype(F32)
    weights = []
    for q in range(n_z):
        here = position[q : q + 1] == slot
        weights.append(jnp.sum(jnp.where(here, cols[q : q + 1], 0.0), axis=1, keepdims=True))
        placing[q * capacity : (q + 1) * capacity, :] = here.astype(F32).astype(BF)
    weight = jnp.concatenate(weights, axis=0)
    chosen = placing[:, :n_tok]
    rows = packed[:, :, :width].reshape(n_tok, width)
    slot_x[...] = dot(chosen, rows).astype(BF)
    rows = packed[:, :, width : 2 * width].reshape(n_tok, width)
    slot_grad[...] = (weight * dot(chosen, rows)).astype(BF)


def pre_kernel(n_hs, rows, *refs):
    weights, outs, refs = refs[:4], refs[4 : 4 + n_hs], refs[4 + n_hs :]
    buffers, sems, hold = refs[:4], refs[4:8], refs[8]
    half = buffers[0].shape[1]
    count = outs[0].shape[0]
    for i, copy in enumerate(fetch(weights, buffers, sems)):
        copy.wait()
        hold[:, i * half : (i + 1) * half] = dot(rows[...], buffers[i][...]).astype(BF)
    me = lax.axis_index("hs")
    for step, out in enumerate(outs):
        start = pl.multiple_of(lax.rem(me + step, n_hs) * count, count)
        out[...] = hold[pl.ds(start, count), :]


def hidden_kernel(rows, w0, w1, out):
    half = w0.shape[0]
    n_hs, count, _ = out.shape
    for i, w in enumerate((w0, w1)):
        part = dot_last(rows[...], w[...]).astype(BF)
        for p in range(n_hs):
            out[p, :, i * half : (i + 1) * half] = part[p * count : (p + 1) * count]


def act_kernel(hidden_parts, *refs):
    pre_parts, out = refs[:-1], refs[-1]
    n_hs, _, hidden = hidden_parts.shape
    total = lambda parts: functools.reduce(lambda a, b: a + b, [v.astype(F32) for v in parts])
    gate_pre = total([p[:, :hidden] for p in pre_parts])
    up_pre = total([p[:, hidden:] for p in pre_parts])
    hidden_grad = total([hidden_parts[i] for i in range(n_hs)])
    gate_grad, up_grad = backprop(gate_pre, up_pre, hidden_grad)
    for i in range(n_hs):
        out[i, :, :hidden] = gate_grad
        out[i, :, hidden:] = up_grad


def input_kernel(both, w0, w1, w2, w3, out):
    half = w0.shape[1]
    n_hs, count, _ = both.shape
    total = None
    for i, w in enumerate((w0, w1, w2, w3)):
        grads = both[:, :, i * half : (i + 1) * half].reshape(n_hs * count, half)
        part = dot_last(grads, w[...])
        total = part if total is None else total + part
    out[...] = total.astype(BF)


def shards(tokens, grad_out, gates, routes, kept, w_gate, w_up, w_down):
    n_grp, n_z, n_hs = (lax.axis_size(axis) for axis in ("grp", "z", "hs"))
    tok_rows, width = tokens.shape
    capacity = 2 * tok_rows * routes.shape[1] // n_z
    total = n_z * capacity
    gate_w, up_w, down_w = w_gate[0], w_up[0], w_down[0]
    half = gate_w.shape[1]
    shape = lambda *dims: jax.ShapeDtypeStruct(dims, BF)

    gate_o, up_o, down_o = (lax.ppermute(w, "core", CORES) for w in (gate_w, up_w, down_w))

    def exchange(blocks, axis):
        return lax.all_to_all(blocks, axis, 0, 0, tiled=True)

    def dispatch(rows):
        return exchange(rows.reshape(n_z, capacity, width), "z").reshape(total, width)

    packed = local_call(
        functools.partial(pack_kernel, n_z),
        shape(n_grp, tok_rows, 2 * width + LANES),
        10**6,
        60,
        (),
        (tokens, grad_out, gates.T, routes.T, kept.T),
    )
    packed = exchange(packed, "grp")
    slot_x, slot_grad, placing = local_call(
        functools.partial(place_kernel, n_z, capacity),
        (shape(total, width), shape(total, width), shape(total, LANES)),
        4 * total * LANES * width,
        24,
        (packed,),
    )
    rows_x = dispatch(slot_x)
    rows_x, slot_grad, gate_o, up_o, down_o = lax.optimization_barrier(
        (rows_x, slot_grad, gate_o, up_o, down_o)
    )
    rows_grad = dispatch(slot_grad)
    pieces = local_call(
        functools.partial(pre_kernel, n_hs),
        (shape(total // n_hs, 4 * half),) * n_hs,
        8 * total * width * half,
        59.5,
        (rows_x,),
        (gate_w, gate_o, up_w, up_o),
        [pltpu.VMEM((total, 4 * half), BF)],
    )
    pre_parts = [pieces[0]] + [
        lax.ppermute(pieces[step], "hs", [(i, (i + step) % n_hs) for i in range(n_hs)])
        for step in range(1, n_hs)
    ]
    rows_grad, *pre_parts = lax.optimization_barrier((rows_grad, *pre_parts))
    hidden_parts = local_call(
        hidden_kernel,
        shape(n_hs, total // n_hs, 2 * half),
        4 * total * width * half,
        48,
        (rows_grad, down_w, down_o),
    )
    hidden_parts = exchange(hidden_parts, "hs")
    both = local_call(
        act_kernel,
        shape(n_hs, total // n_hs, 4 * half),
        20 * total * half,
        24,
        (hidden_parts, *pre_parts),
    )
    both = exchange(both, "hs")
    mine = local_call(
        input_kernel,
        shape(total, width),
        8 * total * width * half,
        48,
        (both, gate_w, gate_o, up_w, up_o),
    )
    returned = dispatch(mine)
    token_rows = lax.dot_general(
        placing[:, : n_grp * tok_rows],
        returned,
        (((0,), (0,)), ((), ())),
        preferred_element_type=F32,
    )
    back_rows = exchange(token_rows.astype(BF).reshape(n_grp, tok_rows, width), "grp")
    return jnp.sum(back_rows.astype(F32), axis=0).astype(BF)


def solution(mesh):
    n_grp, n_exp, n_hs = mesh.devices.shape
    chips = Mesh(
        mesh.devices.reshape(n_grp, n_exp // 2, 2, n_hs), ("grp", "z", "core", "hs")
    )
    rows = ("grp", "z", "core")
    placed = (
        P(rows, "hs"),
        P(rows, "hs"),
        P(rows, None),
        P(rows, None),
        P(rows, None),
        P(rows, "hs", None),
        P(rows, "hs", None),
        P(rows, None, "hs"),
    )
    return jax.shard_map(
        shards, mesh=chips, in_specs=placed, out_specs=P(rows, "hs"), check_vma=False
    )
```

```python
import functools

import jax
import jax.numpy as jnp
from jax import lax
from jax.experimental import pallas as pl
from jax.experimental.pallas import tpu as pltpu
from jax.sharding import Mesh, PartitionSpec as P

BF = jnp.bfloat16
F32 = jnp.float32
LAST = (((1,), (1,)), ((), ()))
CORES = [(0, 1), (1, 0)]
LANES = 128


def backprop(gate_pre, up_pre, hidden_grad):
    sigma = jax.nn.sigmoid(gate_pre)
    slope = sigma * (1.0 + gate_pre * (1.0 - sigma))
    gate_grad = (hidden_grad * up_pre * slope).astype(BF)
    up_grad = (hidden_grad * gate_pre * sigma).astype(BF)
    return (gate_grad, up_grad)


def dot(a, b):
    return jnp.dot(a, b, preferred_element_type=F32)


def dot_last(a, b):
    return lax.dot_general(a, b, LAST, preferred_element_type=F32)


def iota(shape, axis):
    return lax.broadcasted_iota(jnp.int32, shape, axis)


def local_call(kernel, out_shape, flops, vmem, held, fetched=(), scratch=()):
    outs = out_shape if isinstance(out_shape, tuple) else (out_shape,)
    size = sum(v.size * v.dtype.itemsize for v in (*held, *fetched, *outs))
    inside = pl.BlockSpec(memory_space=pltpu.VMEM)
    buffers = [pltpu.VMEM(v.shape, v.dtype) for v in fetched]
    return pl.pallas_call(
        kernel,
        out_shape=out_shape,
        in_specs=[inside] * len(held) + [pl.BlockSpec(memory_space=pltpu.HBM)] * len(fetched),
        out_specs=tuple(inside for _ in outs) if isinstance(out_shape, tuple) else inside,
        scratch_shapes=[*buffers, *[pltpu.SemaphoreType.DMA] * len(fetched), *scratch],
        compiler_params=pltpu.CompilerParams(vmem_limit_bytes=int(vmem * 1024 * 1024)),
        cost_estimate=pl.CostEstimate(flops=flops, bytes_accessed=size, transcendentals=0),
    )(*held, *fetched)


def fetch(sources, buffers, sems):
    copies = [pltpu.make_async_copy(*refs) for refs in zip(sources, buffers, sems)]
    for copy in copies:
        copy.start()
    return copies


def pack_kernel(n_z, *refs):
    out, buffers, sems = refs[5], refs[6:11], refs[11:16]
    copies = fetch(refs[:5], buffers, sems)
    tokens, grads, gates, routes, kept = buffers
    n_grp, tok_rows, _ = out.shape
    width = tokens.shape[1]
    for copy in copies:
        copy.wait()
    place = iota((tok_rows, LANES), 1) == iota((tok_rows, LANES), 0) + lax.axis_index("grp") * tok_rows
    place = place.astype(F32).astype(BF)
    low = lambda v: v.astype(F32).astype(BF)
    used = low(kept[...])
    weight = dot(low(gates[...]) * used, place)
    expert = jnp.where(dot(used, place) > 0.5, dot(low(routes[...]), place), -1.0)
    ids = iota((n_grp * n_z, LANES), 0).astype(F32)
    table = jnp.zeros((n_grp * n_z, LANES), F32)
    for k in range(weight.shape[0]):
        table = table + jnp.where(expert[k : k + 1] == ids, weight[k : k + 1], 0.0)
    table = table.astype(BF)
    if n_z < tok_rows:
        out[:, :, 2 * width :] = jnp.zeros((n_grp, tok_rows, LANES), BF)
    for g in range(n_grp):
        out[g, :, :width] = tokens[...]
        out[g, :, width : 2 * width] = grads[...]
        out[g, :n_z, 2 * width :] = table[g * n_z : (g + 1) * n_z]


def place_kernel(n_z, capacity, packed, slot_x, slot_grad, placing):
    n_grp, tok_rows, _ = packed.shape
    width = slot_x.shape[1]
    n_tok = n_grp * tok_rows
    cols = jnp.zeros((tok_rows, LANES), F32)
    for g in range(n_grp):
        cols = cols + packed[g, :, 2 * width :].astype(F32)
    present = cols != 0.0
    before = (iota((LANES, LANES), 0) < iota((LANES, LANES), 1)).astype(F32).astype(BF)
    position = jnp.where(present, dot(present.astype(F32).astype(BF), before), -1.0)
    slot = iota((capacity, LANES), 0).astype(F32)
    weights = []
    for q in range(n_z):
        here = position[q : q + 1] == slot
        weights.append(jnp.sum(jnp.where(here, cols[q : q + 1], 0.0), axis=1, keepdims=True))
        placing[q * capacity : (q + 1) * capacity, :] = here.astype(F32).astype(BF)
    weight = jnp.concatenate(weights, axis=0)
    chosen = placing[:, :n_tok]
    rows = packed[:, :, :width].reshape(n_tok, width)
    slot_x[...] = dot(chosen, rows).astype(BF)
    rows = packed[:, :, width : 2 * width].reshape(n_tok, width)
    slot_grad[...] = (weight * dot(chosen, rows)).astype(BF)


def pre_kernel(n_hs, rows, w0, w1, w2, w3, *refs):
    outs, hold = refs[:n_hs], refs[n_hs]
    half = w0.shape[1]
    count = outs[0].shape[0]
    for i, w in enumerate((w0, w1, w2, w3)):
        hold[:, i * half : (i + 1) * half] = dot(rows[...], w[...]).astype(BF)
    me = lax.axis_index("hs")
    for step, out in enumerate(outs):
        start = pl.multiple_of(lax.rem(me + step, n_hs) * count, count)
        out[...] = hold[pl.ds(start, count), :]


def hidden_kernel(rows, w0, w1, out):
    half = w0.shape[0]
    n_hs, count, _ = out.shape
    for i, w in enumerate((w0, w1)):
        part = dot_last(rows[...], w[...]).astype(BF)
        for p in range(n_hs):
            out[p, :, i * half : (i + 1) * half] = part[p * count : (p + 1) * count]


def act_kernel(hidden_parts, *refs):
    pre_parts, out = refs[:-1], refs[-1]
    n_hs, _, hidden = hidden_parts.shape
    total = lambda parts: functools.reduce(lambda a, b: a + b, [v.astype(F32) for v in parts])
    gate_pre = total([p[:, :hidden] for p in pre_parts])
    up_pre = total([p[:, hidden:] for p in pre_parts])
    hidden_grad = total([hidden_parts[i] for i in range(n_hs)])
    gate_grad, up_grad = backprop(gate_pre, up_pre, hidden_grad)
    for i in range(n_hs):
        out[i, :, :hidden] = gate_grad
        out[i, :, hidden:] = up_grad


def input_kernel(both, w0, w1, w2, w3, out):
    half = w0.shape[1]
    n_hs, count, _ = both.shape
    total = None
    for i, w in enumerate((w0, w1, w2, w3)):
        grads = both[:, :, i * half : (i + 1) * half].reshape(n_hs * count, half)
        part = dot_last(grads, w[...])
        total = part if total is None else total + part
    out[...] = total.astype(BF)


def shards(tokens, grad_out, gates, routes, kept, w_gate, w_up, w_down):
    n_grp, n_z, n_hs = (lax.axis_size(axis) for axis in ("grp", "z", "hs"))
    tok_rows, width = tokens.shape
    capacity = 2 * tok_rows * routes.shape[1] // n_z
    total = n_z * capacity
    gate_w, up_w, down_w = w_gate[0], w_up[0], w_down[0]
    half = gate_w.shape[1]
    shape = lambda *dims: jax.ShapeDtypeStruct(dims, BF)

    gate_o, up_o, down_o = (lax.ppermute(w, "core", CORES) for w in (gate_w, up_w, down_w))

    def exchange(blocks, axis):
        return lax.all_to_all(blocks, axis, 0, 0, tiled=True)

    def dispatch(rows):
        return exchange(rows.reshape(n_z, capacity, width), "z").reshape(total, width)

    packed = local_call(
        functools.partial(pack_kernel, n_z),
        shape(n_grp, tok_rows, 2 * width + LANES),
        10**6,
        60,
        (),
        (tokens, grad_out, gates.T, routes.T, kept.T),
    )
    packed = exchange(packed, "grp")
    slot_x, slot_grad, placing = local_call(
        functools.partial(place_kernel, n_z, capacity),
        (shape(total, width), shape(total, width), shape(total, LANES)),
        4 * total * LANES * width,
        24,
        (packed,),
    )
    rows_x = dispatch(slot_x)
    rows_x, slot_grad, gate_o, up_o, down_o = lax.optimization_barrier(
        (rows_x, slot_grad, gate_o, up_o, down_o)
    )
    rows_grad = dispatch(slot_grad)
    pieces = local_call(
        functools.partial(pre_kernel, n_hs),
        (shape(total // n_hs, 4 * half),) * n_hs,
        8 * total * width * half,
        52,
        (rows_x, gate_w, gate_o, up_w, up_o),
        (),
        [pltpu.VMEM((total, 4 * half), BF)],
    )
    pre_parts = [pieces[0]] + [
        lax.ppermute(pieces[step], "hs", [(i, (i + step) % n_hs) for i in range(n_hs)])
        for step in range(1, n_hs)
    ]
    rows_grad, *pre_parts = lax.optimization_barrier((rows_grad, *pre_parts))
    hidden_parts = local_call(
        hidden_kernel,
        shape(n_hs, total // n_hs, 2 * half),
        4 * total * width * half,
        50,
        (rows_grad, down_w, down_o),
    )
    hidden_parts = exchange(hidden_parts, "hs")
    both = local_call(
        act_kernel,
        shape(n_hs, total // n_hs, 4 * half),
        20 * total * half,
        24,
        (hidden_parts, *pre_parts),
    )
    both = exchange(both, "hs")
    mine = local_call(
        input_kernel,
        shape(total, width),
        8 * total * width * half,
        48,
        (both, gate_w, gate_o, up_w, up_o),
    )
    returned = dispatch(mine)
    token_rows = lax.dot_general(
        placing[:, : n_grp * tok_rows],
        returned,
        (((0,), (0,)), ((), ())),
        preferred_element_type=F32,
    )
    back_rows = exchange(token_rows.astype(BF).reshape(n_grp, tok_rows, width), "grp")
    return jnp.sum(back_rows.astype(F32), axis=0).astype(BF)


def solution(mesh):
    n_grp, n_exp, n_hs = mesh.devices.shape
    chips = Mesh(
        mesh.devices.reshape(n_grp, n_exp // 2, 2, n_hs), ("grp", "z", "core", "hs")
    )
    rows = ("grp", "z", "core")
    placed = (
        P(rows, "hs"),
        P(rows, "hs"),
        P(rows, None),
        P(rows, None),
        P(rows, None),
        P(rows, "hs", None),
        P(rows, "hs", None),
        P(rows, None, "hs"),
    )
    return jax.shard_map(
        shards, mesh=chips, in_specs=placed, out_specs=P(rows, "hs"), check_vma=False
    )
```

```python
import functools

import jax
import jax.numpy as jnp
from jax import lax
from jax.experimental import pallas as pl
from jax.experimental.pallas import tpu as pltpu
from jax.sharding import Mesh, PartitionSpec as P

BF = jnp.bfloat16
F32 = jnp.float32
LAST = (((1,), (1,)), ((), ()))
CORES = [(0, 1), (1, 0)]
LANES = 128


def backprop(gate_pre, up_pre, hidden_grad):
    sigma = jax.nn.sigmoid(gate_pre)
    slope = sigma * (1.0 + gate_pre * (1.0 - sigma))
    gate_grad = (hidden_grad * up_pre * slope).astype(BF)
    up_grad = (hidden_grad * gate_pre * sigma).astype(BF)
    return (gate_grad, up_grad)


def dot(a, b):
    return jnp.dot(a, b, preferred_element_type=F32)


def dot_last(a, b):
    return lax.dot_general(a, b, LAST, preferred_element_type=F32)


def iota(shape, axis):
    return lax.broadcasted_iota(jnp.int32, shape, axis)


def local_call(kernel, out_shape, flops, vmem, held, fetched=(), scratch=()):
    outs = out_shape if isinstance(out_shape, tuple) else (out_shape,)
    size = sum(v.size * v.dtype.itemsize for v in (*held, *fetched, *outs))
    inside = pl.BlockSpec(memory_space=pltpu.VMEM)
    buffers = [pltpu.VMEM(v.shape, v.dtype) for v in fetched]
    return pl.pallas_call(
        kernel,
        out_shape=out_shape,
        in_specs=[inside] * len(held) + [pl.BlockSpec(memory_space=pltpu.HBM)] * len(fetched),
        out_specs=tuple(inside for _ in outs) if isinstance(out_shape, tuple) else inside,
        scratch_shapes=[*buffers, *[pltpu.SemaphoreType.DMA] * len(fetched), *scratch],
        compiler_params=pltpu.CompilerParams(vmem_limit_bytes=int(vmem * 1024 * 1024)),
        cost_estimate=pl.CostEstimate(flops=flops, bytes_accessed=size, transcendentals=0),
    )(*held, *fetched)


def fetch(sources, buffers, sems):
    copies = [pltpu.make_async_copy(*refs) for refs in zip(sources, buffers, sems)]
    for copy in copies:
        copy.start()
    return copies


def pack_kernel(n_z, *refs):
    out, buffers, sems = refs[5], refs[6:11], refs[11:16]
    copies = fetch(refs[:5], buffers, sems)
    tokens, grads, gates, routes, kept = buffers
    n_grp, tok_rows, _ = out.shape
    width = tokens.shape[1]
    for copy in copies:
        copy.wait()
    place = iota((tok_rows, LANES), 1) == iota((tok_rows, LANES), 0) + lax.axis_index("grp") * tok_rows
    place = place.astype(F32).astype(BF)
    low = lambda v: v.astype(F32).astype(BF)
    used = low(kept[...])
    weight = dot(low(gates[...]) * used, place)
    expert = jnp.where(dot(used, place) > 0.5, dot(low(routes[...]), place), -1.0)
    ids = iota((n_grp * n_z, LANES), 0).astype(F32)
    table = jnp.zeros((n_grp * n_z, LANES), F32)
    for k in range(weight.shape[0]):
        table = table + jnp.where(expert[k : k + 1] == ids, weight[k : k + 1], 0.0)
    table = table.astype(BF)
    if n_z < tok_rows:
        out[:, :, 2 * width :] = jnp.zeros((n_grp, tok_rows, LANES), BF)
    for g in range(n_grp):
        out[g, :, :width] = tokens[...]
        out[g, :, width : 2 * width] = grads[...]
        out[g, :n_z, 2 * width :] = table[g * n_z : (g + 1) * n_z]


def place_kernel(n_z, capacity, packed, slots, placing):
    n_grp, tok_rows, _ = packed.shape
    width = slots.shape[1] // 2
    n_tok = n_grp * tok_rows
    cols = jnp.zeros((tok_rows, LANES), F32)
    for g in range(n_grp):
        cols = cols + packed[g, :, 2 * width :].astype(F32)
    present = cols != 0.0
    before = (iota((LANES, LANES), 0) < iota((LANES, LANES), 1)).astype(F32).astype(BF)
    position = jnp.where(present, dot(present.astype(F32).astype(BF), before), -1.0)
    slot = iota((capacity, LANES), 0).astype(F32)
    weights = []
    for q in range(n_z):
        here = position[q : q + 1] == slot
        weights.append(jnp.sum(jnp.where(here, cols[q : q + 1], 0.0), axis=1, keepdims=True))
        placing[q * capacity : (q + 1) * capacity, :] = here.astype(F32).astype(BF)
    weight = jnp.concatenate(weights, axis=0)
    chosen = placing[:, :n_tok]
    rows = packed[:, :, :width].reshape(n_tok, width)
    slots[:, :width] = dot(chosen, rows).astype(BF)
    rows = packed[:, :, width : 2 * width].reshape(n_tok, width)
    slots[:, width:] = (weight * dot(chosen, rows)).astype(BF)


def parts_kernel(*refs):
    out, (rows, *buffers), sems = refs[7], refs[8:15], refs[15:]
    width, half = buffers[0].shape
    n_hs, count, _ = out.shape
    got_rows, *got_weights = fetch(refs[:7], (rows, *buffers), sems)
    got_rows.wait()
    for i, copy in enumerate(got_weights):
        copy.wait()
        if i < 4:
            part = dot(rows[:, :width], buffers[i][...]).astype(BF)
        else:
            part = dot_last(rows[:, width:], buffers[i][...]).astype(BF)
        for p in range(n_hs):
            out[p, :, i * half : (i + 1) * half] = part[p * count : (p + 1) * count]


def act_kernel(parts, out):
    n_hs, _, hidden = parts.shape
    hidden = hidden // 3
    add = lambda i: functools.reduce(
        lambda a, b: a + b,
        [parts[p, :, i * hidden : (i + 1) * hidden].astype(F32) for p in range(n_hs)],
    )
    gate_grad, up_grad = backprop(add(0), add(1), add(2))
    for i in range(n_hs):
        out[i, :, :hidden] = gate_grad
        out[i, :, hidden:] = up_grad


def input_kernel(both, w0, w1, w2, w3, out):
    half = w0.shape[1]
    n_hs, count, _ = both.shape
    total = None
    for i, w in enumerate((w0, w1, w2, w3)):
        grads = both[:, :, i * half : (i + 1) * half].reshape(n_hs * count, half)
        part = dot_last(grads, w[...])
        total = part if total is None else total + part
    out[...] = total.astype(BF)


def shards(tokens, grad_out, gates, routes, kept, w_gate, w_up, w_down):
    n_grp, n_z, n_hs = (lax.axis_size(axis) for axis in ("grp", "z", "hs"))
    tok_rows, width = tokens.shape
    capacity = 2 * tok_rows * routes.shape[1] // n_z
    total = n_z * capacity
    gate_w, up_w, down_w = w_gate[0], w_up[0], w_down[0]
    half = gate_w.shape[1]
    shape = lambda *dims: jax.ShapeDtypeStruct(dims, BF)

    gate_o, up_o, down_o = (lax.ppermute(w, "core", CORES) for w in (gate_w, up_w, down_w))

    def exchange(blocks, axis):
        return lax.all_to_all(blocks, axis, 0, 0, tiled=True)

    def dispatch(rows):
        return exchange(rows.reshape(n_z, capacity, -1), "z").reshape(total, -1)

    packed = local_call(
        functools.partial(pack_kernel, n_z),
        shape(n_grp, tok_rows, 2 * width + LANES),
        10**6,
        60,
        (),
        (tokens, grad_out, gates.T, routes.T, kept.T),
    )
    packed = exchange(packed, "grp")
    slots, placing = local_call(
        functools.partial(place_kernel, n_z, capacity),
        (shape(total, 2 * width), shape(total, LANES)),
        4 * total * LANES * width,
        24,
        (packed,),
    )
    rows = dispatch(slots)
    parts = local_call(
        parts_kernel,
        shape(n_hs, total // n_hs, 6 * half),
        12 * total * width * half,
        56,
        (),
        (rows, gate_w, gate_o, up_w, up_o, down_w, down_o),
    )
    parts = exchange(parts, "hs")
    both = local_call(
        act_kernel,
        shape(n_hs, total // n_hs, 4 * half),
        20 * total * half,
        24,
        (parts,),
    )
    both = exchange(both, "hs")
    mine = local_call(
        input_kernel,
        shape(total, width),
        8 * total * width * half,
        48,
        (both, gate_w, gate_o, up_w, up_o),
    )
    returned = dispatch(mine)
    token_rows = lax.dot_general(
        placing[:, : n_grp * tok_rows],
        returned,
        (((0,), (0,)), ((), ())),
        preferred_element_type=F32,
    )
    back_rows = exchange(token_rows.astype(BF).reshape(n_grp, tok_rows, width), "grp")
    return jnp.sum(back_rows.astype(F32), axis=0).astype(BF)


def solution(mesh):
    n_grp, n_exp, n_hs = mesh.devices.shape
    chips = Mesh(
        mesh.devices.reshape(n_grp, n_exp // 2, 2, n_hs), ("grp", "z", "core", "hs")
    )
    rows = ("grp", "z", "core")
    placed = (
        P(rows, "hs"),
        P(rows, "hs"),
        P(rows, None),
        P(rows, None),
        P(rows, None),
        P(rows, "hs", None),
        P(rows, "hs", None),
        P(rows, None, "hs"),
    )
    return jax.shard_map(
        shards, mesh=chips, in_specs=placed, out_specs=P(rows, "hs"), check_vma=False
    )
```

```python
import functools

import jax
import jax.numpy as jnp
from jax import lax
from jax.experimental import pallas as pl
from jax.experimental.pallas import tpu as pltpu
from jax.sharding import Mesh, PartitionSpec as P

BF = jnp.bfloat16
F32 = jnp.float32
LAST = (((1,), (1,)), ((), ()))
CORES = [(0, 1), (1, 0)]
LANES = 128


def backprop(gate_pre, up_pre, hidden_grad):
    sigma = jax.nn.sigmoid(gate_pre)
    slope = sigma * (1.0 + gate_pre * (1.0 - sigma))
    gate_grad = (hidden_grad * up_pre * slope).astype(BF)
    up_grad = (hidden_grad * gate_pre * sigma).astype(BF)
    return (gate_grad, up_grad)


def dot(a, b):
    return jnp.dot(a, b, preferred_element_type=F32)


def dot_last(a, b):
    return lax.dot_general(a, b, LAST, preferred_element_type=F32)


def iota(shape, axis):
    return lax.broadcasted_iota(jnp.int32, shape, axis)


def local_call(kernel, out_shape, flops, vmem, held, fetched=(), scratch=()):
    outs = out_shape if isinstance(out_shape, tuple) else (out_shape,)
    size = sum(v.size * v.dtype.itemsize for v in (*held, *fetched, *outs))
    inside = pl.BlockSpec(memory_space=pltpu.VMEM)
    buffers = [pltpu.VMEM(v.shape, v.dtype) for v in fetched]
    return pl.pallas_call(
        kernel,
        out_shape=out_shape,
        in_specs=[inside] * len(held) + [pl.BlockSpec(memory_space=pltpu.HBM)] * len(fetched),
        out_specs=tuple(inside for _ in outs) if isinstance(out_shape, tuple) else inside,
        scratch_shapes=[*buffers, *[pltpu.SemaphoreType.DMA] * len(fetched), *scratch],
        compiler_params=pltpu.CompilerParams(vmem_limit_bytes=int(vmem * 1024 * 1024)),
        cost_estimate=pl.CostEstimate(flops=flops, bytes_accessed=size, transcendentals=0),
    )(*held, *fetched)


def fetch(sources, buffers, sems):
    copies = [pltpu.make_async_copy(*refs) for refs in zip(sources, buffers, sems)]
    for copy in copies:
        copy.start()
    return copies


def pack_kernel(n_z, *refs):
    out, buffers, sems = refs[5], refs[6:11], refs[11:16]
    copies = fetch(refs[:5], buffers, sems)
    tokens, grads, gates, routes, kept = buffers
    n_grp, tok_rows, _ = out.shape
    width = tokens.shape[1]
    for copy in copies:
        copy.wait()
    place = iota((tok_rows, LANES), 1) == iota((tok_rows, LANES), 0) + lax.axis_index("grp") * tok_rows
    place = place.astype(F32).astype(BF)
    low = lambda v: v.astype(F32).astype(BF)
    used = low(kept[...])
    weight = dot(low(gates[...]) * used, place)
    expert = jnp.where(dot(used, place) > 0.5, dot(low(routes[...]), place), -1.0)
    ids = iota((n_grp * n_z, LANES), 0).astype(F32)
    table = jnp.zeros((n_grp * n_z, LANES), F32)
    for k in range(weight.shape[0]):
        table = table + jnp.where(expert[k : k + 1] == ids, weight[k : k + 1], 0.0)
    table = table.astype(BF)
    if n_z < tok_rows:
        out[:, :, 2 * width :] = jnp.zeros((n_grp, tok_rows, LANES), BF)
    for g in range(n_grp):
        out[g, :, :width] = tokens[...]
        out[g, :, width : 2 * width] = grads[...]
        out[g, :n_z, 2 * width :] = table[g * n_z : (g + 1) * n_z]


def place_kernel(n_z, capacity, packed, slot_x, placing, weight):
    n_grp, tok_rows, _ = packed.shape
    width = slot_x.shape[1]
    n_tok = n_grp * tok_rows
    cols = jnp.zeros((tok_rows, LANES), F32)
    for g in range(n_grp):
        cols = cols + packed[g, :, 2 * width :].astype(F32)
    present = cols != 0.0
    before = (iota((LANES, LANES), 0) < iota((LANES, LANES), 1)).astype(F32).astype(BF)
    position = jnp.where(present, dot(present.astype(F32).astype(BF), before), -1.0)
    slot = iota((capacity, LANES), 0).astype(F32)
    for q in range(n_z):
        here = position[q : q + 1] == slot
        found = jnp.sum(jnp.where(here, cols[q : q + 1], 0.0), axis=1, keepdims=True)
        weight[q * capacity : (q + 1) * capacity, :] = jnp.broadcast_to(found, here.shape).astype(BF)
        placing[q * capacity : (q + 1) * capacity, :] = here.astype(F32).astype(BF)
    rows = packed[:, :, :width].reshape(n_tok, width)
    slot_x[...] = dot(placing[:, :n_tok], rows).astype(BF)


def grad_kernel(packed, placing, weight, slot_grad):
    n_grp, tok_rows, _ = packed.shape
    width = slot_grad.shape[1]
    n_tok = n_grp * tok_rows
    rows = packed[:, :, width : 2 * width].reshape(n_tok, width)
    scale = weight[:, :1].astype(F32)
    slot_grad[...] = (scale * dot(placing[:, :n_tok], rows)).astype(BF)


def pre_kernel(n_hs, rows, w0, w1, w2, w3, *refs):
    outs, hold = refs[:n_hs], refs[n_hs]
    half = w0.shape[1]
    count = outs[0].shape[0]
    for i, w in enumerate((w0, w1, w2, w3)):
        hold[:, i * half : (i + 1) * half] = dot(rows[...], w[...]).astype(BF)
    me = lax.axis_index("hs")
    for step, out in enumerate(outs):
        start = pl.multiple_of(lax.rem(me + step, n_hs) * count, count)
        out[...] = hold[pl.ds(start, count), :]


def hidden_kernel(rows, w0, w1, out):
    half = w0.shape[0]
    n_hs, count, _ = out.shape
    for i, w in enumerate((w0, w1)):
        part = dot_last(rows[...], w[...]).astype(BF)
        for p in range(n_hs):
            out[p, :, i * half : (i + 1) * half] = part[p * count : (p + 1) * count]


def act_kernel(hidden_parts, *refs):
    pre_parts, out = refs[:-1], refs[-1]
    n_hs, _, hidden = hidden_parts.shape
    total = lambda parts: functools.reduce(lambda a, b: a + b, [v.astype(F32) for v in parts])
    gate_pre = total([p[:, :hidden] for p in pre_parts])
    up_pre = total([p[:, hidden:] for p in pre_parts])
    hidden_grad = total([hidden_parts[i] for i in range(n_hs)])
    gate_grad, up_grad = backprop(gate_pre, up_pre, hidden_grad)
    for i in range(n_hs):
        out[i, :, :hidden] = gate_grad
        out[i, :, hidden:] = up_grad


def input_kernel(both, w0, w1, w2, w3, out):
    half = w0.shape[1]
    n_hs, count, _ = both.shape
    total = None
    for i, w in enumerate((w0, w1, w2, w3)):
        grads = both[:, :, i * half : (i + 1) * half].reshape(n_hs * count, half)
        part = dot_last(grads, w[...])
        total = part if total is None else total + part
    out[...] = total.astype(BF)


def shards(tokens, grad_out, gates, routes, kept, w_gate, w_up, w_down):
    n_grp, n_z, n_hs = (lax.axis_size(axis) for axis in ("grp", "z", "hs"))
    tok_rows, width = tokens.shape
    capacity = 2 * tok_rows * routes.shape[1] // n_z
    total = n_z * capacity
    gate_w, up_w, down_w = w_gate[0], w_up[0], w_down[0]
    half = gate_w.shape[1]
    shape = lambda *dims: jax.ShapeDtypeStruct(dims, BF)

    gate_o, up_o, down_o = (lax.ppermute(w, "core", CORES) for w in (gate_w, up_w, down_w))

    def exchange(blocks, axis):
        return lax.all_to_all(blocks, axis, 0, 0, tiled=True)

    def dispatch(rows):
        return exchange(rows.reshape(n_z, capacity, width), "z").reshape(total, width)

    packed = local_call(
        functools.partial(pack_kernel, n_z),
        shape(n_grp, tok_rows, 2 * width + LANES),
        10**6,
        60,
        (),
        (tokens, grad_out, gates.T, routes.T, kept.T),
    )
    packed = exchange(packed, "grp")
    slot_x, placing, weight = local_call(
        functools.partial(place_kernel, n_z, capacity),
        (shape(total, width), shape(total, LANES), shape(total, LANES)),
        2 * total * LANES * width,
        24,
        (packed,),
    )
    slot_x, packed = lax.optimization_barrier((slot_x, packed))
    slot_grad = local_call(
        grad_kernel,
        shape(total, width),
        2 * total * LANES * width,
        24,
        (packed, placing, weight),
    )
    rows_x = dispatch(slot_x)
    rows_x, slot_grad, gate_o, up_o, down_o = lax.optimization_barrier(
        (rows_x, slot_grad, gate_o, up_o, down_o)
    )
    rows_grad = dispatch(slot_grad)
    pieces = local_call(
        functools.partial(pre_kernel, n_hs),
        (shape(total // n_hs, 4 * half),) * n_hs,
        8 * total * width * half,
        52,
        (rows_x, gate_w, gate_o, up_w, up_o),
        (),
        [pltpu.VMEM((total, 4 * half), BF)],
    )
    pre_parts = [pieces[0]] + [
        lax.ppermute(pieces[step], "hs", [(i, (i + step) % n_hs) for i in range(n_hs)])
        for step in range(1, n_hs)
    ]
    rows_grad, *pre_parts = lax.optimization_barrier((rows_grad, *pre_parts))
    hidden_parts = local_call(
        hidden_kernel,
        shape(n_hs, total // n_hs, 2 * half),
        4 * total * width * half,
        50,
        (rows_grad, down_w, down_o),
    )
    hidden_parts = exchange(hidden_parts, "hs")
    both = local_call(
        act_kernel,
        shape(n_hs, total // n_hs, 4 * half),
        20 * total * half,
        24,
        (hidden_parts, *pre_parts),
    )
    both = exchange(both, "hs")
    mine = local_call(
        input_kernel,
        shape(total, width),
        8 * total * width * half,
        48,
        (both, gate_w, gate_o, up_w, up_o),
    )
    returned = dispatch(mine)
    token_rows = lax.dot_general(
        placing[:, : n_grp * tok_rows],
        returned,
        (((0,), (0,)), ((), ())),
        preferred_element_type=F32,
    )
    back_rows = exchange(token_rows.astype(BF).reshape(n_grp, tok_rows, width), "grp")
    return jnp.sum(back_rows.astype(F32), axis=0).astype(BF)


def solution(mesh):
    n_grp, n_exp, n_hs = mesh.devices.shape
    chips = Mesh(
        mesh.devices.reshape(n_grp, n_exp // 2, 2, n_hs), ("grp", "z", "core", "hs")
    )
    rows = ("grp", "z", "core")
    placed = (
        P(rows, "hs"),
        P(rows, "hs"),
        P(rows, None),
        P(rows, None),
        P(rows, None),
        P(rows, "hs", None),
        P(rows, "hs", None),
        P(rows, None, "hs"),
    )
    return jax.shard_map(
        shards, mesh=chips, in_specs=placed, out_specs=P(rows, "hs"), check_vma=False
    )
```

```python
import functools

import jax
import jax.numpy as jnp
from jax import lax
from jax.experimental import pallas as pl
from jax.experimental.pallas import tpu as pltpu
from jax.sharding import Mesh, PartitionSpec as P

BF = jnp.bfloat16
F32 = jnp.float32
LAST = (((1,), (1,)), ((), ()))
CORES = [(0, 1), (1, 0)]
LANES = 128


def backprop(gate_pre, up_pre, hidden_grad):
    sigma = jax.nn.sigmoid(gate_pre)
    slope = sigma * (1.0 + gate_pre * (1.0 - sigma))
    gate_grad = (hidden_grad * up_pre * slope).astype(BF)
    up_grad = (hidden_grad * gate_pre * sigma).astype(BF)
    return (gate_grad, up_grad)


def dot(a, b):
    return jnp.dot(a, b, preferred_element_type=F32)


def dot_last(a, b):
    return lax.dot_general(a, b, LAST, preferred_element_type=F32)


def iota(shape, axis):
    return lax.broadcasted_iota(jnp.int32, shape, axis)


def local_call(kernel, out_shape, flops, vmem, held, fetched=(), scratch=()):
    outs = out_shape if isinstance(out_shape, tuple) else (out_shape,)
    size = sum(v.size * v.dtype.itemsize for v in (*held, *fetched, *outs))
    inside = pl.BlockSpec(memory_space=pltpu.VMEM)
    buffers = [pltpu.VMEM(v.shape, v.dtype) for v in fetched]
    return pl.pallas_call(
        kernel,
        out_shape=out_shape,
        in_specs=[inside] * len(held) + [pl.BlockSpec(memory_space=pltpu.HBM)] * len(fetched),
        out_specs=tuple(inside for _ in outs) if isinstance(out_shape, tuple) else inside,
        scratch_shapes=[*buffers, *[pltpu.SemaphoreType.DMA] * len(fetched), *scratch],
        compiler_params=pltpu.CompilerParams(vmem_limit_bytes=int(vmem * 1024 * 1024)),
        cost_estimate=pl.CostEstimate(flops=flops, bytes_accessed=size, transcendentals=0),
    )(*held, *fetched)


def fetch(sources, buffers, sems):
    copies = [pltpu.make_async_copy(*refs) for refs in zip(sources, buffers, sems)]
    for copy in copies:
        copy.start()
    return copies


def pack_kernel(n_z, *refs):
    out, buffers, sems = refs[5], refs[6:11], refs[11:16]
    copies = fetch(refs[:5], buffers, sems)
    tokens, grads, gates, routes, kept = buffers
    n_grp, tok_rows, _ = out.shape
    width = tokens.shape[1]
    for copy in copies:
        copy.wait()
    place = iota((tok_rows, LANES), 1) == iota((tok_rows, LANES), 0) + lax.axis_index("grp") * tok_rows
    place = place.astype(F32).astype(BF)
    low = lambda v: v.astype(F32).astype(BF)
    used = low(kept[...])
    weight = dot(low(gates[...]) * used, place)
    expert = jnp.where(dot(used, place) > 0.5, dot(low(routes[...]), place), -1.0)
    ids = iota((n_grp * n_z, LANES), 0).astype(F32)
    table = jnp.zeros((n_grp * n_z, LANES), F32)
    for k in range(weight.shape[0]):
        table = table + jnp.where(expert[k : k + 1] == ids, weight[k : k + 1], 0.0)
    table = table.astype(BF)
    if n_z < tok_rows:
        out[:, :, 2 * width :] = jnp.zeros((n_grp, tok_rows, LANES), BF)
    for g in range(n_grp):
        out[g, :, :width] = tokens[...]
        out[g, :, width : 2 * width] = grads[...]
        out[g, :n_z, 2 * width :] = table[g * n_z : (g + 1) * n_z]


def place_kernel(n_z, capacity, packed, slot_x, placing, weight):
    n_grp, tok_rows, _ = packed.shape
    width = slot_x.shape[1]
    n_tok = n_grp * tok_rows
    cols = jnp.zeros((tok_rows, LANES), F32)
    for g in range(n_grp):
        cols = cols + packed[g, :, 2 * width :].astype(F32)
    present = cols != 0.0
    before = (iota((LANES, LANES), 0) < iota((LANES, LANES), 1)).astype(F32).astype(BF)
    position = jnp.where(present, dot(present.astype(F32).astype(BF), before), -1.0)
    slot = iota((capacity, LANES), 0).astype(F32)
    for q in range(n_z):
        here = position[q : q + 1] == slot
        found = jnp.sum(jnp.where(here, cols[q : q + 1], 0.0), axis=1, keepdims=True)
        weight[q * capacity : (q + 1) * capacity, :] = jnp.broadcast_to(found, here.shape).astype(BF)
        placing[q * capacity : (q + 1) * capacity, :] = here.astype(F32).astype(BF)
    rows = packed[:, :, :width].reshape(n_tok, width)
    slot_x[...] = dot(placing[:, :n_tok], rows).astype(BF)


def grad_kernel(packed, placing, weight, slot_grad):
    n_grp, tok_rows, _ = packed.shape
    width = slot_grad.shape[1]
    n_tok = n_grp * tok_rows
    rows = packed[:, :, width : 2 * width].reshape(n_tok, width)
    scale = weight[:, :1].astype(F32)
    slot_grad[...] = (scale * dot(placing[:, :n_tok], rows)).astype(BF)


def pre_kernel(n_hs, rows, w0, w2, w1, w3, *refs):
    outs, (b1, b3, s1, s3, hold) = refs[:n_hs], refs[n_hs:]
    half = w0.shape[1]
    count = outs[0].shape[0]
    copies = fetch((w1, w3), (b1, b3), (s1, s3))
    for i, w in ((0, w0), (2, w2), (1, b1), (3, b3)):
        if i % 2:
            copies[i // 2].wait()
        hold[:, i * half : (i + 1) * half] = dot(rows[...], w[...]).astype(BF)
    me = lax.axis_index("hs")
    for step, out in enumerate(outs):
        start = pl.multiple_of(lax.rem(me + step, n_hs) * count, count)
        out[...] = hold[pl.ds(start, count), :]


def hidden_kernel(rows, w0, w1, out, buffer, sem):
    half = w0.shape[0]
    n_hs, count, _ = out.shape
    (copy,) = fetch((w1,), (buffer,), (sem,))
    for i, w in enumerate((w0, buffer)):
        if i == 1:
            copy.wait()
        part = dot_last(rows[...], w[...]).astype(BF)
        for p in range(n_hs):
            out[p, :, i * half : (i + 1) * half] = part[p * count : (p + 1) * count]


def act_kernel(hidden_parts, *refs):
    pre_parts, out = refs[:-1], refs[-1]
    n_hs, _, hidden = hidden_parts.shape
    total = lambda parts: functools.reduce(lambda a, b: a + b, [v.astype(F32) for v in parts])
    gate_pre = total([p[:, :hidden] for p in pre_parts])
    up_pre = total([p[:, hidden:] for p in pre_parts])
    hidden_grad = total([hidden_parts[i] for i in range(n_hs)])
    gate_grad, up_grad = backprop(gate_pre, up_pre, hidden_grad)
    for i in range(n_hs):
        out[i, :, :hidden] = gate_grad
        out[i, :, hidden:] = up_grad


def input_kernel(both, w0, w1, w2, w3, out):
    half = w0.shape[1]
    n_hs, count, _ = both.shape
    total = None
    for i, w in enumerate((w0, w1, w2, w3)):
        grads = both[:, :, i * half : (i + 1) * half].reshape(n_hs * count, half)
        part = dot_last(grads, w[...])
        total = part if total is None else total + part
    out[...] = total.astype(BF)


def shards(tokens, grad_out, gates, routes, kept, w_gate, w_up, w_down):
    n_grp, n_z, n_hs = (lax.axis_size(axis) for axis in ("grp", "z", "hs"))
    tok_rows, width = tokens.shape
    capacity = 2 * tok_rows * routes.shape[1] // n_z
    total = n_z * capacity
    gate_w, up_w, down_w = w_gate[0], w_up[0], w_down[0]
    half = gate_w.shape[1]
    shape = lambda *dims: jax.ShapeDtypeStruct(dims, BF)

    gate_o, up_o, down_o = (lax.ppermute(w, "core", CORES) for w in (gate_w, up_w, down_w))

    def exchange(blocks, axis):
        return lax.all_to_all(blocks, axis, 0, 0, tiled=True)

    def dispatch(rows):
        return exchange(rows.reshape(n_z, capacity, width), "z").reshape(total, width)

    packed = local_call(
        functools.partial(pack_kernel, n_z),
        shape(n_grp, tok_rows, 2 * width + LANES),
        10**6,
        60,
        (),
        (tokens, grad_out, gates.T, routes.T, kept.T),
    )
    packed = exchange(packed, "grp")
    slot_x, placing, weight = local_call(
        functools.partial(place_kernel, n_z, capacity),
        (shape(total, width), shape(total, LANES), shape(total, LANES)),
        2 * total * LANES * width,
        24,
        (packed,),
    )
    slot_x, packed = lax.optimization_barrier((slot_x, packed))
    slot_grad = local_call(
        grad_kernel,
        shape(total, width),
        2 * total * LANES * width,
        24,
        (packed, placing, weight),
    )
    rows_x = dispatch(slot_x)
    rows_x, slot_grad, gate_o, up_o, down_o = lax.optimization_barrier(
        (rows_x, slot_grad, gate_o, up_o, down_o)
    )
    rows_grad = dispatch(slot_grad)
    pieces = local_call(
        functools.partial(pre_kernel, n_hs),
        (shape(total // n_hs, 4 * half),) * n_hs,
        8 * total * width * half,
        52,
        (rows_x, gate_w, up_w),
        (gate_o, up_o),
        [pltpu.VMEM((total, 4 * half), BF)],
    )
    pre_parts = [pieces[0]] + [
        lax.ppermute(pieces[step], "hs", [(i, (i + step) % n_hs) for i in range(n_hs)])
        for step in range(1, n_hs)
    ]
    rows_grad, *pre_parts = lax.optimization_barrier((rows_grad, *pre_parts))
    hidden_parts = local_call(
        hidden_kernel,
        shape(n_hs, total // n_hs, 2 * half),
        4 * total * width * half,
        52,
        (rows_grad, down_w),
        (down_o,),
    )
    hidden_parts = exchange(hidden_parts, "hs")
    both = local_call(
        act_kernel,
        shape(n_hs, total // n_hs, 4 * half),
        20 * total * half,
        24,
        (hidden_parts, *pre_parts),
    )
    both = exchange(both, "hs")
    mine = local_call(
        input_kernel,
        shape(total, width),
        8 * total * width * half,
        48,
        (both, gate_w, gate_o, up_w, up_o),
    )
    returned = dispatch(mine)
    token_rows = lax.dot_general(
        placing[:, : n_grp * tok_rows],
        returned,
        (((0,), (0,)), ((), ())),
        preferred_element_type=F32,
    )
    back_rows = exchange(token_rows.astype(BF).reshape(n_grp, tok_rows, width), "grp")
    return jnp.sum(back_rows.astype(F32), axis=0).astype(BF)


def solution(mesh):
    n_grp, n_exp, n_hs = mesh.devices.shape
    chips = Mesh(
        mesh.devices.reshape(n_grp, n_exp // 2, 2, n_hs), ("grp", "z", "core", "hs")
    )
    rows = ("grp", "z", "core")
    placed = (
        P(rows, "hs"),
        P(rows, "hs"),
        P(rows, None),
        P(rows, None),
        P(rows, None),
        P(rows, "hs", None),
        P(rows, "hs", None),
        P(rows, None, "hs"),
    )
    return jax.shard_map(
        shards, mesh=chips, in_specs=placed, out_specs=P(rows, "hs"), check_vma=False
    )
```
